32 devices in a mesh: dp: 8 (over y, x, core), seq: 4 (over z).
Axes of the slice: x: 2, y: 2, z: 4, core: 2. Of those that a mesh axis runs over, the one named last changes fastest.
Arguments:
- hidden_in: bfloat16 [8, 2048, 2048], P('dp', 'seq'), may hold values from -6 to 6
- positions: int32 [8, 2048], P('dp', 'seq'), may hold values from 0 to 6141, as said below
- cotangent: bfloat16 [8, 2048, 2048], P('dp', 'seq'), may hold values from -6 to 6
- input_projection: float32 [2048, 4096], P(('dp', 'seq')), may hold values from -0.125 to 0.125
- out_proj: float32 [2048, 2048], P(('dp', 'seq')), may hold values from -1 to 1
- gate_up: float32 [2048, 12288], P(('dp', 'seq')), may hold values from -0.125 to 0.125
- down_proj: float32 [2048, 6144], P(('dp', 'seq')), may hold values from -0.078125 to 0.078125
- gains: float32 [4352], P(('dp', 'seq')), may hold values from 0.5 to 1.5
- input_first_moment: float32 [2048, 4096], P(('dp', 'seq')), may hold values from -32 to 32
- input_second_moment: float32 [2048, 4096], P(('dp', 'seq')), may hold values from 137.6256 to 557.056
- out_first: float32 [2048, 2048], P(('dp', 'seq')), may hold values from -6 to 6
- out_second: float32 [2048, 2048], P(('dp', 'seq')), may hold values from 4.25984 to 16.384
- gate_first: float32 [2048, 12288], P(('dp', 'seq')), may hold values from -32 to 32
- gate_second: float32 [2048, 12288], P(('dp', 'seq')), may hold values from 104.8576 to 425.984
- down_first: float32 [2048, 6144], P(('dp', 'seq')), may hold values from -48 to 48
- down_second: float32 [2048, 6144], P(('dp', 'seq')), may hold values from 311.296 to 1245.184
- gain_first: float32 [4352], P(('dp', 'seq')), may hold values from -64 to 64
- gain_second: float32 [4352], P(('dp', 'seq')), may hold values from 557.056 to 2211.84
Outputs:
- layer_out: bfloat16 [8, 2048, 2048], P('dp', 'seq')
- input_grad: float32 [8, 2048, 2048], P('dp', 'seq')
- in_proj_new: float32 [2048, 4096], P(('dp', 'seq'))
- in_first_new: float32 [2048, 4096], P(('dp', 'seq'))
- in_second_new: float32 [2048, 4096], P(('dp', 'seq'))
- out_proj_new: float32 [2048, 2048], P(('dp', 'seq'))
- out_first_new: float32 [2048, 2048], P(('dp', 'seq'))
- out_second_new: float32 [2048, 2048], P(('dp', 'seq'))
- gate_up_new: float32 [2048, 12288], P(('dp', 'seq'))
- gate_first_new: float32 [2048, 12288], P(('dp', 'seq'))
- gate_second_new: float32 [2048, 12288], P(('dp', 'seq'))
- down_proj_new: float32 [2048, 6144], P(('dp', 'seq'))
- down_first_new: float32 [2048, 6144], P(('dp', 'seq'))
- down_second_new: float32 [2048, 6144], P(('dp', 'seq'))
- gains_new: float32 [4352], P(('dp', 'seq'))
- gain_first_new: float32 [4352], P(('dp', 'seq'))
- gain_second_new: float32 [4352], P(('dp', 'seq'))
The draws below stay inside these ranges and needn't reach their ends.
Inputs may be any that keep to these rules, and one draw needn't show every extreme that they name: Within each sequence, positions start at 0 and rise by 1 to 3 from one token to the next.
All inputs are finite; a program needn't handle non-finite values.
Results may differ from the reference program's by a relative error of at most 0.014.
The reference program's roundings to bfloat16 on the way count: a program that leaves them out, or rounds other values in their place, can miss the bound.
Values may be sent and summed in bfloat16 or wider, within the bound.
No kernel may reach another device: no remote copies, remote signals or barrier semaphores. Data moves between devices by JAX's collectives and lax.ppermute only.
A program may use at most 512 MiB of HBM per device.

```python
import math
import jax
import jax.numpy as jnp
from jax import lax

MODEL_WIDTH = 2048
QUERY_HEADS = 16
KEY_VALUE_HEADS = 8
HEAD_SIZE = 128
FF = 6144
LENGTH = 2048
STEP = 10
SEQUENCES = 8
TOKEN_TOTAL = 16384
GAINS = 4352


def draw_positions(key, part):
    key = jax.random.fold_in(key, 7)
    step_key, pick_key = jax.random.split(key)
    increments = jax.random.randint(step_key, (SEQUENCES, LENGTH), 1, 4)
    chosen = jax.random.randint(pick_key, (), 0, SEQUENCES)
    rows = jnp.arange(SEQUENCES, dtype=jnp.int32)[:, None]
    increments = jnp.where(rows == chosen, 3, increments)
    increments = increments * (jnp.arange(LENGTH, dtype=jnp.int32) > 0).astype(jnp.int32)[None, :]
    return jnp.cumsum(increments, axis=1).astype(jnp.int32)


def block_levels(own_key, dims, pieces, least, largest):
    def one(dim, blocks):
        draws = jax.random.uniform(jax.random.fold_in(jax.random.fold_in(own_key, 6), dim), (blocks,), jnp.float32, least / len(pieces), largest / len(pieces))
        return jnp.repeat(jnp.exp(draws), dims[dim] // blocks).reshape((-1,) + (1,) * (len(dims) - dim - 1))

    gain = one(*pieces[0])
    for cut in pieces[1:]:
        gain = gain * one(*cut)
    return gain


def noise(own_key, shape, scale, limit, pieces=(), kind=jnp.bfloat16):
    gain = block_levels(own_key, shape, pieces, -0.22, 0.18) if pieces else 1.0
    values = jax.random.normal(own_key, shape, jnp.float32) * scale * gain
    return jnp.minimum(jnp.maximum(values, -limit), limit).astype(kind)


def setup_inputs(seed: int = 0) -> dict:
    arg_keys = jax.random.split(jax.random.key(seed), 19)
    return {
        "hidden_in": noise(arg_keys[0], (SEQUENCES, LENGTH, MODEL_WIDTH), 1.0, 6.0, ((0, 8), (1, 4))),
        "positions": draw_positions(jax.random.fold_in(arg_keys[18], 71), 0),
        "cotangent": noise(arg_keys[2], (SEQUENCES, LENGTH, MODEL_WIDTH), 1.0, 6.0, ((0, 8), (1, 4))),
        "input_projection": noise(arg_keys[3], (MODEL_WIDTH, (QUERY_HEADS + 2 * KEY_VALUE_HEADS) * HEAD_SIZE), MODEL_WIDTH ** -0.5, 0.125, ((0, 32),), jnp.float32),
        "out_proj": noise(arg_keys[4], (MODEL_WIDTH, QUERY_HEADS * HEAD_SIZE), (QUERY_HEADS * HEAD_SIZE // 64) ** -0.5, 1.0, ((0, 32),), jnp.float32),
        "gate_up": noise(arg_keys[5], (MODEL_WIDTH, 2 * FF), MODEL_WIDTH ** -0.5, 0.125, ((0, 32),), jnp.float32),
        "down_proj": noise(arg_keys[6], (MODEL_WIDTH, FF), FF ** -0.5, 0.078125, ((0, 32),), jnp.float32),
        "gains": jnp.clip(1.0 + 0.1 * jax.random.normal(arg_keys[7], (GAINS,), jnp.float32), 0.5, 1.5),
        "input_first_moment": noise(arg_keys[8], (MODEL_WIDTH, (QUERY_HEADS + 2 * KEY_VALUE_HEADS) * HEAD_SIZE), (0.044 * TOKEN_TOTAL ** 0.5), 32.0, ((0, 32),), jnp.float32),
        "input_second_moment": jnp.clip(jnp.exp(math.log(557.056) - 1.3981289 * jax.random.uniform(arg_keys[9], (MODEL_WIDTH, (QUERY_HEADS + 2 * KEY_VALUE_HEADS) * HEAD_SIZE), jnp.float32) ** block_levels(arg_keys[9], (MODEL_WIDTH, (QUERY_HEADS + 2 * KEY_VALUE_HEADS) * HEAD_SIZE), ((0, 32),), -0.2, 0.2)), 137.6256, 557.056),
        "out_first": noise(arg_keys[10], (MODEL_WIDTH, QUERY_HEADS * HEAD_SIZE), (0.0078 * TOKEN_TOTAL ** 0.5), 6.0, ((0, 32),), jnp.float32),
        "out_second": jnp.clip(jnp.exp(math.log(16.384) - 1.3470737 * jax.random.uniform(arg_keys[11], (MODEL_WIDTH, QUERY_HEADS * HEAD_SIZE), jnp.float32) ** block_levels(arg_keys[11], (MODEL_WIDTH, QUERY_HEADS * HEAD_SIZE), ((0, 32),), -0.2, 0.2)), 4.25984, 16.384),
        "gate_first": noise(arg_keys[12], (MODEL_WIDTH, 2 * FF), (0.039 * TOKEN_TOTAL ** 0.5), 32.0, ((0, 32),), jnp.float32),
        "gate_second": jnp.clip(jnp.exp(math.log(425.984) - 1.4017986 * jax.random.uniform(arg_keys[13], (MODEL_WIDTH, 2 * FF), jnp.float32) ** block_levels(arg_keys[13], (MODEL_WIDTH, 2 * FF), ((0, 32),), -0.2, 0.2)), 104.8576, 425.984),
        "down_first": noise(arg_keys[14], (MODEL_WIDTH, FF), (0.067 * TOKEN_TOTAL ** 0.5), 48.0, ((0, 32),), jnp.float32),
        "down_second": jnp.clip(jnp.exp(math.log(1245.184) - 1.3862944 * jax.random.uniform(arg_keys[15], (MODEL_WIDTH, FF), jnp.float32) ** block_levels(arg_keys[15], (MODEL_WIDTH, FF), ((0, 32),), -0.2, 0.2)), 311.296, 1245.184),
        "gain_first": noise(arg_keys[16], (GAINS,), (0.089 * TOKEN_TOTAL ** 0.5), 64.0, ((0, 32),), jnp.float32),
        "gain_second": jnp.clip(jnp.exp(math.log(2211.84) - 1.3789142 * jax.random.uniform(arg_keys[17], (GAINS,), jnp.float32) ** block_levels(arg_keys[17], (GAINS,), ((0, 32),), -0.2, 0.2)), 557.056, 2211.84),
    }


norm_eps = 1e-06
rope_base = 1000000.0
beta_one = 0.9
beta_two = 0.95
adam_eps = 1e-08
weight_decay = 0.1
masked_score = -1e+30

@jax.custom_vjp
def reduced_input(v):
    return lax.optimization_barrier(v.astype(jnp.bfloat16)).astype(jnp.float32)

@jax.custom_vjp
def reduced_backward(v):
    return v

def low_keep(v):
    return (reduced_input(v), None)

def low_pass(kept, grad):
    return (grad,)

def back_keep(v):
    return (v, None)

def back_low(kept, grad):
    return (reduced_input(grad),)
reduced_input.defvjp(low_keep, low_pass)
reduced_backward.defvjp(back_keep, back_low)

def product(left, right):
    return jnp.dot(left, right, precision=lax.Precision.HIGHEST, preferred_element_type=jnp.float32)

def rms_normed(values):
    return values * lax.rsqrt(lax.optimization_barrier(jnp.mean(values * values, axis=-1, keepdims=True)) + norm_eps)

def rotary_tables(places, extent):
    half_dim = extent // 2
    freqs = jnp.exp(jnp.arange(half_dim, dtype=jnp.float32) * (-2.0 * math.log(rope_base) / extent))
    angles = places.astype(jnp.float32)[:, None] * freqs[None, :]
    return (jnp.cos(angles), jnp.sin(angles))

def rotate(values, cosine_table, sine_table):
    half_dim = values.shape[-1] // 2
    first_half = values[..., :half_dim]
    second_half = values[..., half_dim:]
    cos_wide = cosine_table[:, None, :]
    sin_wide = sine_table[:, None, :]
    return jnp.concatenate([first_half * cos_wide - second_half * sin_wide, second_half * cos_wide + first_half * sin_wide], axis=-1)

def attention_ref(queries, keys, values):
    sequence_length = queries.shape[0]
    head_repeat_count = QUERY_HEADS // KEY_VALUE_HEADS
    keys_wide = jnp.repeat(keys, head_repeat_count, axis=1)
    values_wide = jnp.repeat(values, head_repeat_count, axis=1)
    block_rows = min(512, sequence_length)
    block_count = sequence_length // block_rows
    score_scale = HEAD_SIZE ** (-0.5)

    def one_block(index):
        offset = index * block_rows
        query_block = lax.dynamic_slice_in_dim(queries, offset, block_rows, 0)
        scores = jnp.einsum('qhd,khd->hqk', query_block, keys_wide, precision=lax.Precision.HIGHEST)
        scores = reduced_backward(scores * score_scale)
        causal = (offset + jnp.arange(block_rows, dtype=jnp.int32))[:, None] >= jnp.arange(sequence_length, dtype=jnp.int32)[None, :]
        scores = jnp.where(causal[None], scores, masked_score)
        highest = lax.optimization_barrier(jnp.max(scores, axis=-1, keepdims=True))
        expd = jnp.exp(scores - highest)
        probs = expd / lax.optimization_barrier(jnp.sum(expd, axis=-1, keepdims=True))
        return jnp.einsum('hqk,khd->qhd', reduced_input(probs), values_wide, precision=lax.Precision.HIGHEST)
    blocks = lax.map(jax.checkpoint(one_block), jnp.arange(block_count, dtype=jnp.int32))
    return blocks.reshape(sequence_length, QUERY_HEADS, HEAD_SIZE)

def layer_forward(inputs, input_projection, out_proj, gate_up, down_proj, gains, places):
    sequence_length = inputs.shape[0]
    query_width = QUERY_HEADS * HEAD_SIZE
    key_width = KEY_VALUE_HEADS * HEAD_SIZE
    gain_all = reduced_input(gains)
    gain_attn = gain_all[:MODEL_WIDTH]
    gain_mlp = gain_all[MODEL_WIDTH:2 * MODEL_WIDTH]
    gain_query = gain_all[2 * MODEL_WIDTH:2 * MODEL_WIDTH + HEAD_SIZE]
    gain_key = gain_all[2 * MODEL_WIDTH + HEAD_SIZE:]
    attn_in = reduced_input(rms_normed(inputs) * gain_attn)
    projected_rows = product(attn_in, reduced_input(input_projection))
    query_raw = reduced_backward(projected_rows[:, :query_width]).reshape(sequence_length, QUERY_HEADS, HEAD_SIZE)
    key_unrotated = reduced_backward(projected_rows[:, query_width:query_width + key_width]).reshape(sequence_length, KEY_VALUE_HEADS, HEAD_SIZE)
    value_per_head = reduced_input(reduced_backward(projected_rows[:, query_width + key_width:])).reshape(sequence_length, KEY_VALUE_HEADS, HEAD_SIZE)
    cosine_table, sine_table = rotary_tables(places, HEAD_SIZE)
    queries = reduced_input(reduced_backward(rotate(rms_normed(query_raw) * gain_query, cosine_table, sine_table)))
    keys = reduced_input(reduced_backward(rotate(rms_normed(key_unrotated) * gain_key, cosine_table, sine_table)))
    attended = reduced_input(reduced_backward(attention_ref(queries, keys, value_per_head)))
    attn_out = reduced_backward(product(attended.reshape(sequence_length, query_width), reduced_input(out_proj).T))
    residual = inputs + attn_out
    mlp_in = reduced_input(rms_normed(residual) * gain_mlp)
    gate_up_raw = product(mlp_in, reduced_input(gate_up))
    gate_pre = reduced_backward(gate_up_raw[:, :FF])
    up_pre = reduced_backward(gate_up_raw[:, FF:])
    hidden = reduced_input(jax.nn.silu(gate_pre) * up_pre)
    return residual + product(hidden, reduced_input(down_proj).T)

def adamw_update(param, gradient, first, second, rate, decay):
    first = beta_one * first + (1.0 - beta_one) * gradient
    second = beta_two * second + (1.0 - beta_two) * gradient * gradient
    first_hat = first / (1.0 - beta_one ** STEP)
    second_hat = second / (1.0 - beta_two ** STEP)
    param = param - rate * (first_hat / (jnp.sqrt(second_hat) + adam_eps) + decay * param)
    return (param, first, second)

def reference(hidden_in, positions, cotangent, input_projection, out_proj, gate_up, down_proj, gains, input_first_moment, input_second_moment, out_first, out_second, gate_first, gate_second, down_first, down_second, gain_first, gain_second):
    params = (input_projection, out_proj, gate_up, down_proj, gains)

    def one_sequence(totals, element):
        inputs, places, upstream = element
        outputs, pull = jax.vjp(lambda values, *weights: layer_forward(values, *weights, places), inputs, *params)
        grads = pull(upstream)
        totals = tuple((total + gradient for total, gradient in zip(totals, grads[1:])))
        return (totals, (outputs, grads[0]))
    zeros = tuple((jnp.zeros_like(param) for param in params))
    totals, (outputs, input_grad) = lax.scan(one_sequence, zeros, (hidden_in.astype(jnp.float32), positions, cotangent.astype(jnp.float32)))
    in_new = adamw_update(input_projection, totals[0], input_first_moment, input_second_moment, 1.0 / math.sqrt(MODEL_WIDTH), weight_decay)
    out_new = adamw_update(out_proj, totals[1], out_first, out_second, 8.0 / math.sqrt(QUERY_HEADS * HEAD_SIZE), weight_decay)
    gate_new = adamw_update(gate_up, totals[2], gate_first, gate_second, 1.0 / math.sqrt(MODEL_WIDTH), weight_decay)
    down_new = adamw_update(down_proj, totals[3], down_first, down_second, 1.0 / math.sqrt(FF), weight_decay)
    gain_new = adamw_update(gains, totals[4], gain_first, gain_second, 0.5, 0.0)
    return (outputs.astype(jnp.bfloat16), input_grad, in_new[0], in_new[1], in_new[2], out_new[0], out_new[1], out_new[2], gate_new[0], gate_new[1], gate_new[2], down_new[0], down_new[1], down_new[2], gain_new[0], gain_new[1], gain_new[2])
```

```python
import functools
import math
import jax
import jax.numpy as jnp
from jax import lax
from jax.sharding import Mesh
from jax.sharding import PartitionSpec as P
from jax.experimental import pallas as pl
from jax.experimental.pallas import tpu as pltpu

HEAD_SIZE = 128
REPEATS = 2
SLOTS = 4
norm_eps = 1e-06
masked_score = -1e30
MIB = 1024 * 1024
LOG2E = 1.4426950408889634


def params(mib):
    return pltpu.CompilerParams(vmem_limit_bytes=mib * MIB)


def dot(left, right, left_dim, right_dim):
    return lax.dot_general(
        left, right, (((left_dim,), (right_dim,)), ((), ())), preferred_element_type=jnp.float32
    )


def head(slot):
    return slice(slot * HEAD_SIZE, (slot + 1) * HEAD_SIZE)


def rotary_forward_kernel(query_ref, key_ref, value_ref, cos_ref, sin_ref, gain_ref, out_ref):
    cosine, sine = cos_ref[...], sin_ref[...]
    for slot in range(REPEATS + 1):
        values = query_ref[:, head(slot)] if slot < REPEATS else key_ref[...]
        _, values = normed_rows(values)
        values = values * gain_ref[slot][None, :]
        values = values * cosine + pltpu.roll(values, HEAD_SIZE // 2, 1) * sine
        out_ref[0, :, head(slot)] = values.astype(jnp.bfloat16)
    out_ref[0, :, head(REPEATS + 1)] = value_ref[...].astype(jnp.bfloat16)


def rotary_forward(raw, cosine, sine, gain_heads, part, count):
    rows, width = raw.shape
    tokens, wide = rows // 2, SLOTS * HEAD_SIZE
    every = width // wide
    groups = every // count
    start = part * groups
    return pl.pallas_call(
        rotary_forward_kernel,
        grid=(2, groups),
        in_specs=[
            pl.BlockSpec((tokens, REPEATS * HEAD_SIZE), lambda s, g: (s, start + g)),
            pl.BlockSpec((tokens, HEAD_SIZE), lambda s, g: (s, every * REPEATS + start + g)),
            pl.BlockSpec((tokens, HEAD_SIZE), lambda s, g: (s, every * (REPEATS + 1) + start + g)),
            pl.BlockSpec((tokens, HEAD_SIZE), lambda s, g: (s, 0)),
            pl.BlockSpec((tokens, HEAD_SIZE), lambda s, g: (s, 0)),
            pl.BlockSpec(gain_heads.shape, lambda s, g: (0, 0)),
        ],
        out_specs=pl.BlockSpec((1, tokens, wide), lambda s, g: (s * groups + g, 0, 0)),
        out_shape=jax.ShapeDtypeStruct((2 * groups, tokens, wide), jnp.bfloat16),
        compiler_params=params(24),
        cost_estimate=pl.CostEstimate(flops=0, bytes_accessed=rows * width, transcendentals=0),
        name="rotary_forward",
    )(raw, raw, raw, cosine, sine, gain_heads)


def rotary_backward_kernel(count, *refs):
    grad_refs = refs[:count]
    raw_ref, cos_ref, sin_ref, gain_ref, out_ref, sum_ref = refs[count:]
    groups = grad_refs[0].shape[0]

    @pl.when(pl.program_id(0) == 0)
    def _():
        sum_ref[...] = jnp.zeros_like(sum_ref)

    cosine, sine = cos_ref[...], sin_ref[...]
    every = count * groups
    for part in range(count):
        for group in range(groups):
            for slot in range(SLOTS):
                grad = grad_refs[part][group, :, head(slot)]
                at = part * groups + group
                columns = head(at * REPEATS + slot if slot < REPEATS else every * slot + at)
                if slot <= REPEATS:
                    grad = grad.astype(jnp.float32)
                    grad = grad * cosine - pltpu.roll(grad, HEAD_SIZE // 2, 1) * sine
                    values = raw_ref[:, columns]
                    scale, normed = normed_rows(values)
                    product = grad * normed
                    sum_ref[slot, :] += jnp.sum(product, axis=0)
                    gain = gain_ref[slot][None, :]
                    inner = jnp.mean(product * gain, axis=-1, keepdims=True)
                    grad = (scale * (grad * gain - normed * inner)).astype(jnp.bfloat16)
                out_ref[:, columns] = grad


def rotary_backward(grads, raw, cosine, sine, gain_heads):
    rows, width = raw.shape
    groups, tokens, wide = grads[0].shape
    block = min(256, tokens)
    steps = tokens // block
    table = pl.BlockSpec((block, HEAD_SIZE), lambda i: (i, 0))
    return pl.pallas_call(
        functools.partial(rotary_backward_kernel, len(grads)),
        grid=(2 * steps,),
        in_specs=[
            pl.BlockSpec((groups // 2, block, wide), lambda i: (i // steps, i % steps, 0))
            for _ in grads
        ]
        + [
            pl.BlockSpec((block, width), lambda i: (i, 0)),
            table,
            table,
            pl.BlockSpec(gain_heads.shape, lambda i: (0, 0)),
        ],
        out_specs=[
            pl.BlockSpec((block, width), lambda i: (i, 0)),
            pl.BlockSpec((8, HEAD_SIZE), lambda i: (0, 0)),
        ],
        out_shape=[
            jax.ShapeDtypeStruct((rows, width), jnp.bfloat16),
            jax.ShapeDtypeStruct((8, HEAD_SIZE), jnp.float32),
        ],
        compiler_params=params(32),
        cost_estimate=pl.CostEstimate(flops=0, bytes_accessed=rows * width, transcendentals=0),
        name="rotary_backward",
    )(*grads, raw, cosine, sine, gain_heads)


def to_columns_kernel(*refs):
    out_ref = refs[-1]
    width = refs[0].shape[2]
    at = 0
    for ref in refs[:-1]:
        for group in range(ref.shape[0]):
            out_ref[:, at : at + width] = ref[group]
            at += width


def to_columns(parts):
    groups, tokens, width = parts[0].shape
    wide = len(parts) * groups // 2 * width
    return pl.pallas_call(
        to_columns_kernel,
        grid=(2,),
        in_specs=[pl.BlockSpec((groups // 2, tokens, width), lambda s: (s, 0, 0)) for _ in parts],
        out_specs=pl.BlockSpec((tokens, wide), lambda s: (s, 0)),
        out_shape=jax.ShapeDtypeStruct((2 * tokens, wide), parts[0].dtype),
        compiler_params=params(16),
        cost_estimate=pl.CostEstimate(flops=0, bytes_accessed=tokens * wide, transcendentals=0),
        name="to_columns",
    )(*parts)


def from_columns_kernel(values_ref, *out_refs):
    width = out_refs[0].shape[2]
    at = 0
    for ref in out_refs:
        for group in range(ref.shape[0]):
            ref[group] = values_ref[:, at : at + width]
            at += width


def from_columns(values, count, groups):
    rows, wide = values.shape
    tokens, width = rows // 2, wide // (count * groups)
    return pl.pallas_call(
        from_columns_kernel,
        grid=(2,),
        in_specs=[pl.BlockSpec((tokens, wide), lambda s: (s, 0))],
        out_specs=[pl.BlockSpec((groups, tokens, width), lambda s: (s, 0, 0))] * count,
        out_shape=[jax.ShapeDtypeStruct((2 * groups, tokens, width), values.dtype)] * count,
        compiler_params=params(16),
        cost_estimate=pl.CostEstimate(flops=0, bytes_accessed=tokens * wide, transcendentals=0),
        name="from_columns",
    )(values)


def causal_mask(scores):
    keys = lax.broadcasted_iota(jnp.int32, scores.shape, 0)
    queries = lax.broadcasted_iota(jnp.int32, scores.shape, 1)
    return keys <= queries


def attend_kernel(query_ref, other_ref, out_ref, sums_ref):
    block = pl.program_id(1)
    scaling = HEAD_SIZE ** (-0.5) * LOG2E

    def step(index, carry, diagonal):
        keys = other_ref[index, 0, :, head(0)]
        values = other_ref[index, 0, :, head(1)]
        result = []
        for repeat in range(REPEATS):
            queries = query_ref[0, 0, :, head(repeat)]
            scores = dot(keys, queries, 1, 1) * scaling
            if diagonal:
                scores = jnp.where(causal_mask(scores), scores, masked_score)
            highest = jnp.max(scores, axis=0, keepdims=True)
            if not diagonal:
                old_highest, old_total, old_sums = carry[repeat]
                highest = jnp.maximum(highest, old_highest)
            weights = jnp.exp2(scores - highest)
            total = jnp.sum(weights, axis=0, keepdims=True)
            sums = dot(values, weights.astype(jnp.bfloat16), 0, 0)
            if not diagonal:
                rescale = jnp.exp2(old_highest - highest)
                total = total + old_total * rescale
                sums = sums + old_sums * rescale
            result.append((highest, total, sums))
        return tuple(result)

    carry = step(block, None, True)
    carry = lax.fori_loop(0, block, lambda index, now: step(index, now, False), carry)
    for repeat in range(REPEATS):
        highest, total, sums = carry[repeat]
        out_ref[0, 0, :, head(repeat)] = (sums / total).T.astype(jnp.bfloat16)
        sums_ref[0, 0, repeat, :] = (highest + jnp.log2(total))[0]


def attend(parts):
    blocks, units, tokens, _ = parts.shape
    wide = REPEATS * HEAD_SIZE
    return pl.pallas_call(
        attend_kernel,
        grid=(units, blocks),
        in_specs=[
            pl.BlockSpec((1, 1, tokens, wide), lambda u, i: (i, u, 0, 0)),
            pl.BlockSpec((blocks, 1, tokens, wide), lambda u, i: (0, u, 0, 1)),
        ],
        out_specs=[
            pl.BlockSpec((1, 1, tokens, wide), lambda u, i: (i, u, 0, 0)),
            pl.BlockSpec((1, 1, REPEATS, tokens), lambda u, i: (u, i, 0, 0)),
        ],
        out_shape=[
            jax.ShapeDtypeStruct((blocks, units, tokens, wide), jnp.bfloat16),
            jax.ShapeDtypeStruct((units, blocks, REPEATS, tokens), jnp.float32),
        ],
        compiler_params=params(32),
        cost_estimate=pl.CostEstimate(flops=0, bytes_accessed=parts.size, transcendentals=0),
        name="attend",
    )(parts, parts)


def attend_back_kernel(parts_ref, up_ref, attended_ref, sums_ref, out_ref, query_acc, key_acc, value_acc, inner_ref):
    blocks, tokens = parts_ref.shape[0], parts_ref.shape[2]
    scaling = HEAD_SIZE ** (-0.5)
    query_acc[...] = jnp.zeros_like(query_acc)

    def inners(index, _):
        for repeat in range(REPEATS):
            product = up_ref[index, 0, :, head(repeat)].astype(jnp.float32) * attended_ref[
                index, 0, :, head(repeat)
            ].astype(jnp.float32)
            inner_ref[index, repeat, :] = jnp.sum(product.T, axis=0)
        return 0

    lax.fori_loop(0, blocks, inners, 0)

    def pair(key_block, query_block, diagonal):
        keys = parts_ref[key_block, 0, :, head(REPEATS)]
        values = parts_ref[key_block, 0, :, head(REPEATS + 1)]
        for repeat in range(REPEATS):
            queries = parts_ref[query_block, 0, :, head(repeat)]
            upstream = up_ref[query_block, 0, :, head(repeat)]
            scores = dot(keys, queries, 1, 1) * (scaling * LOG2E)
            probs = jnp.exp2(scores - sums_ref[0, query_block, repeat, :][None, :])
            if diagonal:
                probs = jnp.where(causal_mask(probs), probs, 0.0)
            grads = dot(values, upstream, 1, 1)
            grads = (probs * (grads - inner_ref[query_block, repeat, :][None, :])).astype(
                jnp.bfloat16
            )
            value_acc[...] += dot(probs.astype(jnp.bfloat16), upstream, 1, 0)
            key_acc[...] += dot(grads, queries, 1, 0)
            query_acc[query_block, :, head(repeat)] += dot(grads, keys, 0, 0)

    def column(key_block, _):
        key_acc[...] = jnp.zeros_like(key_acc)
        value_acc[...] = jnp.zeros_like(value_acc)
        pair(key_block, key_block, True)

        def later(query_block, _):
            pair(key_block, query_block, False)
            return 0

        lax.fori_loop(key_block + 1, blocks, later, 0)
        out_ref[key_block, 0, :, head(REPEATS)] = (key_acc[...] * scaling).astype(jnp.bfloat16)
        out_ref[key_block, 0, :, head(REPEATS + 1)] = value_acc[...].astype(jnp.bfloat16)
        return 0

    lax.fori_loop(0, blocks, column, 0)
    out_ref[:, 0, :, : REPEATS * HEAD_SIZE] = (query_acc[...] * scaling).astype(jnp.bfloat16)


def attend_back(parts, upstream, attended, log_sums):
    blocks, units, tokens, wide = parts.shape
    half = REPEATS * HEAD_SIZE
    whole = pl.BlockSpec((blocks, 1, tokens, wide), lambda u: (0, u, 0, 0))
    part = pl.BlockSpec((blocks, 1, tokens, half), lambda u: (0, u, 0, 0))
    return pl.pallas_call(
        attend_back_kernel,
        grid=(units,),
        in_specs=[
            whole,
            part,
            part,
            pl.BlockSpec((1, blocks, REPEATS, tokens), lambda u: (u, 0, 0, 0)),
        ],
        out_specs=whole,
        out_shape=jax.ShapeDtypeStruct(parts.shape, jnp.bfloat16),
        scratch_shapes=[
            pltpu.VMEM((blocks, tokens, half), jnp.float32),
            pltpu.VMEM((tokens, HEAD_SIZE), jnp.float32),
            pltpu.VMEM((tokens, HEAD_SIZE), jnp.float32),
            pltpu.VMEM((blocks, REPEATS, tokens), jnp.float32),
        ],
        compiler_params=params(44),
        cost_estimate=pl.CostEstimate(
            flops=0,
            bytes_accessed=parts.size,
            transcendentals=0,
        ),
        name="attend_back",
    )(parts, upstream, attended, log_sums)


def mixed_tiles(values):
    low_half = lax.broadcasted_iota(jnp.int32, (values.shape[0], HEAD_SIZE), 1) < HEAD_SIZE // 2
    tiles = [values[:, head(at)] for at in range(values.shape[1] // HEAD_SIZE)]
    rolled = [pltpu.roll(tile, HEAD_SIZE // 2, 1) for tile in tiles]
    result = []
    for at in range(0, len(tiles), 4):
        for upper, lower in ((at, at + 2), (at + 1, at + 3)):
            result.append(jnp.where(low_half, tiles[upper], rolled[lower]))
            result.append(jnp.where(low_half, rolled[upper], tiles[lower]))
    return jnp.concatenate(result, axis=1)


def unmixed_tiles(values):
    low_half = lax.broadcasted_iota(jnp.int32, (values.shape[0], HEAD_SIZE), 1) < HEAD_SIZE // 2
    tiles = [values[:, head(at)] for at in range(values.shape[1] // HEAD_SIZE)]
    rolled = [pltpu.roll(tile, HEAD_SIZE // 2, 1) for tile in tiles]
    result = []
    for at in range(0, len(tiles), 4):
        upper = [jnp.where(low_half, tiles[at + k], rolled[at + k + 1]) for k in (0, 2)]
        lower = [jnp.where(low_half, rolled[at + k], tiles[at + k + 1]) for k in (0, 2)]
        result += upper + lower
    return jnp.concatenate(result, axis=1)


def loaded(ref, mixed):
    values = ref[...].astype(jnp.float32)
    return mixed_tiles(values) if mixed else values


def normed_rows(values):
    scale = lax.rsqrt(jnp.mean(values * values, axis=-1, keepdims=True) + norm_eps)
    return scale, values * scale


def back_rows(values, gradient, gain):
    scale, normed = normed_rows(values)
    product = gradient * normed
    inner = jnp.mean(product * gain, axis=-1, keepdims=True)
    return scale * (gradient * gain - normed * inner), jnp.sum(product, axis=0, keepdims=True)


def prepare_kernel(mixed, hidden_ref, up_ref, gain_ref, out_ref, up_out_ref):
    _, normed = normed_rows(loaded(hidden_ref, mixed))
    out_ref[...] = (normed * gain_ref[...]).astype(jnp.bfloat16)
    up_out_ref[...] = loaded(up_ref, mixed).astype(jnp.bfloat16)


def middle_kernel(mixed, hidden_ref, own_ref, other_ref, gain_ref, residual_ref, out_ref):
    residual = loaded(hidden_ref, mixed) + (own_ref[...] + other_ref[...].astype(jnp.float32))
    residual_ref[...] = residual
    _, normed = normed_rows(residual)
    out_ref[...] = (normed * gain_ref[...]).astype(jnp.bfloat16)


def outgoing_kernel(mixed, residual_ref, own_ref, other_ref, out_ref):
    result = residual_ref[...] + (own_ref[...] + other_ref[...].astype(jnp.float32))
    if mixed:
        result = unmixed_tiles(result)
    out_ref[...] = result.astype(jnp.bfloat16)


def middle_back_kernel(
    own_ref, other_ref, residual_ref, up_ref, gain_ref, grad_ref, low_ref, sum_ref
):
    @pl.when(pl.program_id(0) == 0)
    def _():
        sum_ref[...] = jnp.zeros_like(sum_ref)

    gradient = own_ref[...] + other_ref[...].astype(jnp.float32)
    back, sums = back_rows(residual_ref[...], gradient, gain_ref[...])
    sum_ref[...] += sums
    back = up_ref[...].astype(jnp.float32) + back
    grad_ref[...] = back
    low_ref[...] = back.astype(jnp.bfloat16)


def incoming_back_kernel(
    mixed, own_ref, other_ref, hidden_ref, later_ref, gain_ref, grad_ref, sum_ref
):
    @pl.when(pl.program_id(0) == 0)
    def _():
        sum_ref[...] = jnp.zeros_like(sum_ref)

    gradient = own_ref[...] + other_ref[...].astype(jnp.float32)
    back, sums = back_rows(loaded(hidden_ref, mixed), gradient, gain_ref[...])
    sum_ref[...] += sums
    back = later_ref[...] + back
    grad_ref[...] = unmixed_tiles(back) if mixed else back


def row_kernel(kernel, operands, results):
    rows, width = operands[0].shape
    block = min(128, rows)

    def spec(shape):
        if shape[0] == 1:
            return pl.BlockSpec((1, width), lambda i: (0, 0))
        return pl.BlockSpec((block, width), lambda i: (i, 0))

    return pl.pallas_call(
        kernel,
        grid=(rows // block,),
        in_specs=[spec(operand.shape) for operand in operands],
        out_specs=[spec((count, width)) for count, _ in results],
        out_shape=[jax.ShapeDtypeStruct((count, width), kind) for count, kind in results],
        compiler_params=params(40),
        cost_estimate=pl.CostEstimate(flops=0, bytes_accessed=rows * width, transcendentals=0),
        name="rows",
    )(*operands)


def sums_kernel(place_ref, left_ref, right_ref, *refs):
    total = dot(left_ref[...], right_ref[...], 1, 0)
    for ref in refs[:-1]:
        total = total + ref[...].astype(jnp.float32)
    refs[-1][...] = total.astype(jnp.bfloat16)


def column_tile(width):
    return 512 if width % 512 == 0 else width


def block_sums(places, left, right, half, *added):
    rows, depth = left.shape
    block, width = rows // 4, right.shape[1] // 2
    count = places.shape[0]
    tile = column_tile(width)
    steps = width // tile
    return pl.pallas_call(
        sums_kernel,
        grid_spec=pltpu.PrefetchScalarGridSpec(
            num_scalar_prefetch=1,
            grid=(count, steps),
            in_specs=[
                pl.BlockSpec((block, depth), lambda i, j, at: (at[i], 0)),
                pl.BlockSpec((depth, tile), lambda i, j, at: (0, half * steps + j)),
            ]
            + [
                pl.BlockSpec((block, tile), functools.partial(lambda which, i, j, at: (which, j), which))
                for _, which in added
            ],
            out_specs=pl.BlockSpec((block, tile), lambda i, j, at: (i, j)),
        ),
        out_shape=jax.ShapeDtypeStruct((count * block, width), jnp.bfloat16),
        compiler_params=params(24),
        cost_estimate=pl.CostEstimate(flops=0, bytes_accessed=block * width, transcendentals=0),
        name="block_sums",
    )(places, left, right, *(array for array, _ in added))


def own_sums_kernel(steps, place_ref, left_ref, right_ref, *refs):
    out_ref = refs[-1]
    total = dot(left_ref[...], right_ref[...], 1, 0)
    first = refs[0][...].astype(jnp.float32) + refs[1][...].astype(jnp.float32)
    second = refs[2][...].astype(jnp.float32) + refs[3][...].astype(jnp.float32)
    total = total + jnp.where(pl.program_id(0) < steps, first, second)
    out_ref[...] = total.astype(jnp.bfloat16)


def own_sums(place, left, right, first, second):
    rows, depth = left.shape
    block, width = rows // 4, right.shape[1] // 2
    tile = column_tile(width)
    steps = width // tile

    def part(which, column):
        return pl.BlockSpec((block, tile), lambda j, at: (which, column(j)))

    return pl.pallas_call(
        functools.partial(own_sums_kernel, steps),
        grid_spec=pltpu.PrefetchScalarGridSpec(
            num_scalar_prefetch=1,
            grid=(2 * steps,),
            in_specs=[
                pl.BlockSpec((block, depth), lambda j, at: (at[0], 0)),
                pl.BlockSpec((depth, tile), lambda j, at: (0, j)),
            ]
            + [part(which, lambda j: jnp.minimum(j, steps - 1)) for _, which in first]
            + [part(which, lambda j: jnp.maximum(j - steps, 0)) for _, which in second],
            out_specs=pl.BlockSpec((block, tile), lambda j, at: (0, j)),
        ),
        out_shape=jax.ShapeDtypeStruct((block, 2 * width), jnp.bfloat16),
        compiler_params=params(24),
        cost_estimate=pl.CostEstimate(flops=0, bytes_accessed=block * width, transcendentals=0),
        name="own_sums",
    )(place, left, right, *(array for array, _ in (*first, *second)))


def partial_kernel(count, *refs):
    own_ref, other_ref = refs[-2:]
    total = dot(refs[0][...], refs[count][...], 1, 1)
    for at in range(1, count):
        total = total + dot(refs[at][...], refs[count + at][...], 1, 1)
    rows = own_ref.shape[0]
    own_ref[...] = total[:rows]
    other_ref[...] = total[rows:].astype(jnp.bfloat16)


def partial_sums(values, weights):
    rows, width = values[0].shape[0], weights[0].shape[0]
    tile = 256
    halves = pl.BlockSpec((rows // 2, tile), lambda j: (0, j))
    return pl.pallas_call(
        functools.partial(partial_kernel, len(values)),
        grid=(width // tile,),
        in_specs=[pl.BlockSpec(value.shape, lambda j: (0, 0)) for value in values]
        + [pl.BlockSpec((tile, weight.shape[1]), lambda j: (j, 0)) for weight in weights],
        out_specs=[halves, halves],
        out_shape=[
            jax.ShapeDtypeStruct((rows // 2, width), jnp.float32),
            jax.ShapeDtypeStruct((rows // 2, width), jnp.bfloat16),
        ],
        compiler_params=params(48),
        cost_estimate=pl.CostEstimate(flops=0, bytes_accessed=rows * width, transcendentals=0),
        name="partial_sums",
    )(*values, *weights)


MODEL_WIDTH = 2048
QUERY_HEADS = 16
KEY_VALUE_HEADS = 8
FF = 6144
STEP = 10

rope_base = 1000000.0
beta_one = 0.9
beta_two = 0.95
adam_eps = 1e-08
weight_decay = 0.1

CORES = 2
COLUMNS = 2
EVERY = ("row", "col", "core", "seq")


def rotary_tables(places):
    half_dim = HEAD_SIZE // 2
    freqs = jnp.exp(
        jnp.arange(half_dim, dtype=jnp.float32) * (-2.0 * math.log(rope_base) / HEAD_SIZE)
    )
    angles = places.astype(jnp.float32)[:, None] * freqs[None, :]
    cosine, sine = jnp.cos(angles), jnp.sin(angles)
    return (
        jnp.concatenate([cosine, cosine], axis=1),
        jnp.concatenate([-sine, sine], axis=1),
    )


def contract_rows(left, right):
    return dot(left, right, 0, 0)


def times(left, right):
    return dot(left, right, 1, 0)


def times_transposed(left, right):
    return dot(left, right, 1, 1)


def low(values):
    return values.astype(jnp.bfloat16)


def full(values):
    return values.astype(jnp.float32)


def shift(values, axis, distance):
    size = lax.axis_size(axis)
    return lax.ppermute(values, axis, [(at, (at + distance) % size) for at in range(size)])


def after(values, *earlier):
    if not earlier:
        return values
    return lax.optimization_barrier((values,) + earlier)[0]


def both_cores(values):
    return jnp.concatenate([values, shift(values, "core", 1)], axis=0)


def own_pair(part, core, spans):
    def half(which):
        pieces = [
            low(lax.dynamic_slice_in_dim(part, start + which * (width // 2), width // 2, 1))
            for start, width in spans
        ]
        return pieces[0] if len(pieces) == 1 else jnp.concatenate(pieces, axis=1)

    kept, received = half(core), shift(half(1 - core), "core", 1)
    return jnp.concatenate(
        [jnp.where(core == 0, kept, received), jnp.where(core == 0, received, kept)], axis=0
    )


def own_rows(pair, core, spans):
    rows = pair.shape[0] // 2
    top, bottom = low(pair[:rows]), low(pair[rows:])
    kept = jnp.where(core == 0, top, bottom)
    received = shift(jnp.where(core == 0, bottom, top), "core", 1)
    halves = jnp.where(core == 0, kept, received), jnp.where(core == 0, received, kept)
    pieces, at = [], 0
    for _, width in spans:
        pieces += [half[:, at : at + width // 2] for half in halves]
        at += width // 2
    return full(jnp.concatenate(pieces, axis=1))


class Plan:
    def __init__(self):
        self.sent, self.arrived, self.pending, self.before = [], [], [], []

    def send(self, values, axis, pairs=((0, 1), (1, 0))):
        result = lax.ppermute(after(values, *self.arrived), axis, pairs)
        self.sent.append(result)
        return result

    def close(self, *also):
        if self.sent or also:
            self.arrived = self.pending = self.sent + list(also)
        self.sent = []

    def now(self, value):
        return after(value, *self.arrived)

    def wait(self, value):
        value = after(value, *self.before, *self.pending)
        self.pending = []
        return value

    def step(self, work, value):
        result = work(self.wait(value))
        self.before = [result]
        return result


def linked():
    return tuple(lax.axis_size(axis) for axis in ("row", "col", "seq")) == (2, 2, 4)


class Gather:
    def __init__(self, plan, pair):
        self.plan, self.pair, self.linked = plan, pair, linked()
        self.parts = []

    def a(self):
        if self.linked:
            other = self.plan.send(self.pair, "seq", ((0, 1), (1, 0), (2, 3), (3, 2)))
            even = lax.axis_index("seq") % 2 == 0
            self.near = jnp.concatenate(
                [jnp.where(even, self.pair, other), jnp.where(even, other, self.pair)], axis=0
            )
            self.parts.append((0, 0, 0, self.near))

    def b(self):
        if self.linked:
            self.middle = self.plan.send(self.near, "seq", ((1, 2), (2, 1)))

    def c(self):
        if self.linked:
            outer = self.plan.send(self.middle, "seq", ((1, 0), (2, 3)))
            seq = lax.axis_index("seq")
            self.far = jnp.where((seq == 1) | (seq == 2), self.middle, outer)
            self.parts.append((0, 0, 1, self.far))

    def near_x(self):
        if self.linked:
            self.near_across = self.plan.send(self.near, "col")
            self.parts.append((0, 1, 0, self.near_across))

    def near_y(self):
        if self.linked:
            self.parts.append((1, 0, 0, self.plan.send(self.near, "row")))

    def near_xy(self):
        if self.linked:
            self.parts.append((1, 1, 0, self.plan.send(self.near_across, "row")))

    def far_x(self):
        if self.linked:
            self.parts.append((0, 1, 1, self.plan.send(self.far, "col")))

    def far_y(self):
        if self.linked:
            self.far_below = self.plan.send(self.far, "row")
            self.parts.append((1, 0, 1, self.far_below))

    def far_yx(self):
        if self.linked:
            self.parts.append((1, 1, 1, self.plan.send(self.far_below, "col")))

    def whole(self, *earlier):
        if not self.linked:
            return lax.all_gather(self.pair, ("row", "col", "seq"), axis=0, tiled=True)
        places = tuple(part[:3] for part in self.parts)
        operands = [part[3] for part in self.parts]
        operands = lax.optimization_barrier((*operands, *earlier))[: len(operands)]
        height, width = self.near.shape
        shape = (height * len(operands), width)
        anywhere = pl.BlockSpec(memory_space=pl.ANY)
        return pl.pallas_call(
            functools.partial(assemble_kernel, places),
            in_specs=[anywhere] * len(operands),
            out_specs=anywhere,
            out_shape=jax.ShapeDtypeStruct(shape, jnp.bfloat16),
            scratch_shapes=[
                pltpu.VMEM(shape, jnp.bfloat16),
                pltpu.SemaphoreType.DMA((len(places),)),
                pltpu.SemaphoreType.DMA((len(places),)),
            ],
            compiler_params=params(shape[0] * shape[1] * 2 // MIB + 4),
            cost_estimate=pl.CostEstimate(
                flops=0, bytes_accessed=shape[0] * shape[1], transcendentals=0
            ),
            name="assemble",
        )(*operands)


def assemble_kernel(places, *refs):
    out_ref, staging, load_sems, store_sems = refs[-4:]
    row, col, seq = lax.axis_index("row"), lax.axis_index("col"), lax.axis_index("seq")
    loads, stores = [], []
    for number, (down, across, other) in enumerate(places):
        height = refs[number].shape[0]
        plane = lax.rem(row + down, 2) * 2 + lax.rem(col + across, 2)
        half = lax.rem(lax.div(seq, 2) + other, 2)
        start = pl.multiple_of((plane * 2 + half) * height, height)
        staged = staging.at[pl.ds(number * height, height)]
        loads.append(pltpu.make_async_copy(refs[number], staged, load_sems.at[number]))
        target = out_ref.at[pl.ds(start, height)]
        stores.append(pltpu.make_async_copy(staged, target, store_sems.at[number]))
    for load in loads:
        load.start()
    for load, store in zip(loads, stores):
        load.wait()
        store.start()
    for store in stores:
        store.wait()


class Scatter:
    def __init__(self, plan, left, right):
        self.plan, self.left, self.right, self.linked = plan, left, right, linked()

    def sums(self, half, *places_and_added):
        places = [step for step in places_and_added if not hasattr(step[0], "dtype")]
        added = [step for step in places_and_added if hasattr(step[0], "dtype")]
        row, col = lax.axis_index("row"), lax.axis_index("col")
        where = jnp.stack([(row + down) % 2 * 2 + (col + across) % 2 for down, across in places])
        return self.plan.step(
            lambda value: block_sums(value, self.left, self.right, half, *added),
            where.astype(jnp.int32),
        )

    def prepare(self):
        if self.linked:
            self.to_send = self.sums(0, (1, 1), (0, 1)), self.sums(1, (1, 1), (1, 0))

    def crossing(self):
        if self.linked:
            self.to_cross = self.sums(0, (1, 1)), self.sums(1, (1, 1))

    def straight(self):
        if self.linked:
            self.to_go = self.sums(0, (0, 1)), self.sums(1, (1, 0))

    def send(self):
        if self.linked:
            came = self.plan.send(self.to_send[0], "col"), self.plan.send(self.to_send[1], "row")
            self.crossed = [(part, 0) for part in came]
            self.straight = [(part, 1) for part in came]

    def send_crossing(self):
        if self.linked:
            came = self.plan.send(self.to_cross[0], "col"), self.plan.send(self.to_cross[1], "row")
            self.crossed = [(part, 0) for part in came]

    def send_straight(self):
        if self.linked:
            came = self.plan.send(self.to_go[0], "col"), self.plan.send(self.to_go[1], "row")
            self.straight = [(part, 0) for part in came]

    def turn(self):
        if self.linked:
            self.to_turn = (
                self.sums(0, (1, 0), self.crossed[0]),
                self.sums(1, (0, 1), self.crossed[1]),
            )

    def send_turned(self):
        if self.linked:
            came = self.plan.send(self.to_turn[0], "row"), self.plan.send(self.to_turn[1], "col")
            self.turned = [(part, 0) for part in came]

    def last(self):
        if not self.linked:
            return low(dot(self.left, self.right, 1, 0))
        first, second = zip(self.straight, self.turned)
        place = (lax.axis_index("row") * 2 + lax.axis_index("col")).astype(jnp.int32)[None]
        return self.plan.step(
            lambda value: own_sums(value, self.left, self.right, first, second), place
        )


def scatter_last(own):
    axes = ("seq",) if linked() else ("row", "col", "seq")
    return lax.psum_scatter(own, axes, scatter_dimension=0, tiled=True)


def adamw_update(param, gradient, first, second, rate, decay):
    first = beta_one * first + (1.0 - beta_one) * gradient
    second = beta_two * second + (1.0 - beta_two) * gradient * gradient
    first_hat = first / (1.0 - beta_one**STEP)
    second_hat = second / (1.0 - beta_two**STEP)
    param = param - rate * (first_hat / (jnp.sqrt(second_hat) + adam_eps) + decay * param)
    return (param, first, second)


def per_device(
    hidden_in,
    positions,
    cotangent,
    input_projection,
    out_proj,
    gate_up,
    down_proj,
    gains,
    input_first_moment,
    input_second_moment,
    out_first,
    out_second,
    gate_first,
    gate_second,
    down_first,
    down_second,
    gain_first,
    gain_second,
):
    core = lax.axis_index("core")
    quads, depth = lax.axis_size("row") * lax.axis_size("col"), lax.axis_size("seq")
    devices = quads * CORES * depth
    _, tokens, width = hidden_in.shape
    rows = width // devices
    groups = KEY_VALUE_HEADS // CORES
    count = 2 * groups // depth
    part_groups = groups // count
    mixed_order = linked() and rows == HEAD_SIZE // CORES

    def to_gathered(values):
        return (
            values.reshape(-1, quads, CORES, depth, rows)
            .transpose(0, 1, 3, 2, 4)
            .reshape(values.shape)
        )

    def from_gathered(values):
        return (
            values.reshape(-1, quads, depth, CORES, rows)
            .transpose(0, 1, 3, 2, 4)
            .reshape(values.shape)
        )

    plan = Plan()
    key_width = KEY_VALUE_HEADS * HEAD_SIZE
    in_spans = (
        (0, REPEATS * key_width),
        (REPEATS * key_width, key_width),
        ((REPEATS + 1) * key_width, key_width),
    )
    gate_span, up_span = (0, FF), (FF, FF)
    out_span, down_span = (0, out_proj.shape[1]), (0, FF)
    in_pair = own_pair(input_projection, core, in_spans)
    in_gather = Gather(plan, in_pair)
    in_gather.a()
    gains_low = lax.all_to_all(
        jnp.broadcast_to(low(gains)[None], (devices, gains.shape[0])),
        EVERY,
        split_axis=0,
        concat_axis=0,
        tiled=True,
    ).reshape(-1)
    plan.close(gains_low)

    in_gather.near_x(), in_gather.near_y(), in_gather.b()
    gate_pair = own_pair(plan.now(gate_up), core, [gate_span])
    gate_gather = Gather(plan, gate_pair)
    out_gather = Gather(plan, own_pair(after(out_proj, gate_pair), core, [out_span]))
    gate_gather.a(), out_gather.a()
    plan.close()

    in_gather.near_xy(), in_gather.c(), gate_gather.b(), gate_gather.near_x()
    plan.close()

    in_gather.far_x(), gate_gather.near_y(), gate_gather.c(), out_gather.b()
    up_pair = own_pair(plan.now(gate_up), core, [up_span])
    up_gather = Gather(plan, up_pair)
    down_pair = own_pair(plan.now(down_proj), core, [down_span])
    down_gather = Gather(plan, down_pair)
    plan.close(up_pair, down_pair)

    gate_gather.far_x(), in_gather.far_y(), up_gather.a(), down_gather.a()
    gain_all = full(gains_low)
    gain_attn = to_gathered(gain_all[:width])[None]
    gain_mlp = to_gathered(gain_all[width : 2 * width])[None]
    gain_query = gain_all[2 * width : 2 * width + HEAD_SIZE]
    gain_key = gain_all[2 * width + HEAD_SIZE :]
    gain_heads = jnp.stack([gain_query] * REPEATS + [gain_key])
    hidden_own, upstream_own = plan.now(hidden_in[0]), cotangent[0]
    if not mixed_order:
        hidden_own, upstream_own = to_gathered(hidden_own), to_gathered(upstream_own)
    attn_own, upstream_own = row_kernel(
        functools.partial(prepare_kernel, mixed_order),
        [hidden_own, upstream_own, gain_attn],
        [(tokens, jnp.bfloat16)] * 2,
    )
    plan.close(attn_own)

    in_gather.far_yx(), gate_gather.far_y(), up_gather.b(), out_gather.c()
    attn_in = both_cores(plan.now(attn_own))
    cosine, sine = rotary_tables(both_cores(positions[0]))
    plan.close(attn_in, cosine, sine)

    def exchange(values):
        return lax.all_to_all(values, "seq", split_axis=0, concat_axis=0, tiled=True)

    def to_heads(values):
        return exchange(values)[:, None]

    def to_tokens(values):
        return exchange(values[:, 0])

    gate_gather.far_yx(), gate_gather.near_xy(), up_gather.c(), down_gather.b()
    in_low = in_gather.whole()
    projected = times(plan.now(attn_in), in_low)
    parts = [
        rotary_forward(projected, cosine, sine, gain_heads, part, count) for part in range(count)
    ]
    plan.close(*parts)

    up_gather.near_x(), up_gather.near_y(), out_gather.near_x(), out_gather.near_y()
    head_parts = [to_heads(plan.now(parts[0]))]
    plan.close(head_parts[0])

    up_gather.far_x(), up_gather.far_y(), out_gather.far_x(), out_gather.far_y()
    attended, log_sums, returned = [], [], []

    def attention(part):
        result, sums = attend(plan.now(head_parts[part]))
        attended.append(result)
        log_sums.append(sums)

    if count == 2:
        head_parts.append(to_heads(plan.now(parts[1])))
    attention(0)
    plan.close(head_parts[-1], attended[0])

    up_gather.far_yx(), up_gather.near_xy(), out_gather.far_yx(), out_gather.near_xy()
    down_gather.c()
    returned.append(to_tokens(plan.now(attended[0])))
    if count == 2:
        attention(1)
    plan.close(attended[-1])

    down_gather.near_x(), down_gather.near_y()
    if count == 2:
        returned.append(to_tokens(plan.now(attended[1])))
    gate_low, up_low = gate_gather.whole(*plan.arrived), up_gather.whole(*plan.arrived)
    upstream = both_cores(plan.now(upstream_own))
    attn_turned, upstream_turned = plan.now(attn_in).T, upstream.T
    plan.close(*returned, gate_low, up_low, upstream)

    down_gather.far_x(), down_gather.far_y()
    mixed = to_columns([plan.now(values) for values in returned])
    out_low = out_gather.whole()
    own, other = partial_sums([mixed], [out_low])
    plan.close(own)

    down_gather.far_yx(), down_gather.near_xy()
    residual, mlp_own = row_kernel(
        functools.partial(middle_kernel, mixed_order),
        [hidden_own, own, shift(plan.now(other), "core", 1), gain_mlp],
        [(tokens, jnp.float32), (tokens, jnp.bfloat16)],
    )
    mlp_low = both_cores(mlp_own)
    gate_pre = times(mlp_low, gate_low)
    up_pre = times(after(mlp_low, gate_pre, attn_turned, upstream_turned), up_low)
    mlp_turned = after(mlp_low, up_pre).T
    down_low = down_gather.whole(up_pre)
    gate_sig = jax.nn.sigmoid(gate_pre)
    gate_act = gate_pre * gate_sig
    hidden = low(gate_act * up_pre)
    grad_hidden = times(upstream, down_low)
    grad_gate = low(grad_hidden * up_pre * gate_sig * (1.0 + gate_pre * (1.0 - gate_sig)))
    grad_up = low(grad_hidden * gate_act)

    plan = Plan()
    down_scatter = Scatter(plan, upstream_turned, hidden)
    gate_scatter = Scatter(plan, mlp_turned, grad_gate)
    up_scatter = Scatter(plan, mlp_turned, grad_up)

    down_scatter.crossing()
    down_scatter.send_crossing()
    down_scatter.straight()
    own, other = partial_sums([plan.wait(grad_gate), grad_up], [gate_low, up_low])
    plan.before = [other]
    plan.close(own)

    down_scatter.send_straight()
    grad_residual, grad_attn_own, sum_g_mlp = row_kernel(
        middle_back_kernel,
        [own, shift(plan.now(other), "core", 1), residual, upstream_own, gain_mlp],
        [(tokens, jnp.float32), (tokens, jnp.bfloat16), (1, jnp.float32)],
    )
    down_scatter.turn()
    gate_scatter.crossing()
    gate_scatter.straight()
    plan.close(grad_attn_own, *plan.before)

    down_scatter.send_turned()
    grad_attn_out = both_cores(plan.now(grad_attn_own))
    grad_attended = low(times(grad_attn_out, out_low))
    plan.close(grad_attended)

    gate_scatter.send_crossing()
    grad_attended = from_columns(grad_attended, count, part_groups)
    grad_heads = [to_heads(grad_attended[0])]
    if count == 2:
        grad_heads.append(to_heads(after(grad_attended[1], grad_heads[0])))
    up_scatter.crossing()
    up_scatter.straight()
    out_scatter = Scatter(plan, grad_attn_out.T, mixed)
    out_scatter.prepare()
    plan.close(*plan.before, grad_heads[0])

    gate_scatter.send_straight()
    grad_parts = []

    def attention_back(part):
        return plan.step(
            lambda value: attend_back(head_parts[part], value, attended[part], log_sums[part]),
            grad_heads[part],
        )

    grad_part = attention_back(0)
    gate_scatter.turn()
    plan.close(*plan.before)

    gate_scatter.send_turned()
    grad_parts.append(to_tokens(grad_part))
    if count == 2:
        grad_part = attention_back(1)
    down_own = down_scatter.last()
    plan.close(*plan.before, grad_parts[0])

    up_scatter.send_crossing()
    out_scatter.send()
    if count == 2:
        grad_parts.append(to_tokens(plan.now(grad_part)))
    mlp_own, mlp_other = partial_sums([plan.wait(hidden)], [down_low])
    plan.before = [mlp_other]
    gate_own = gate_scatter.last()
    plan.close(*plan.before, grad_parts[-1])

    up_scatter.send_straight()
    out_scatter.turn()
    out_scatter.send_turned()
    up_scatter.turn()
    down_sum = scatter_last(plan.now(down_own))
    gate_sum = scatter_last(plan.now(gate_own))
    plan.close(*plan.before)

    up_scatter.send_turned()
    grad_projected, head_gain_sums = rotary_backward(
        [plan.wait(values) for values in grad_parts], projected, cosine, sine, gain_heads
    )
    plan.before = [grad_projected]
    sum_g_query = jnp.sum(head_gain_sums[:REPEATS], axis=0)
    sum_g_key = head_gain_sums[REPEATS]
    in_scatter = Scatter(plan, attn_turned, grad_projected)
    in_scatter.prepare()
    out_own = out_scatter.last()
    plan.close(*plan.before)

    in_scatter.send()
    (layer_out,) = row_kernel(
        functools.partial(outgoing_kernel, mixed_order),
        [residual, mlp_own, shift(plan.now(mlp_other), "core", 1)],
        [(tokens, jnp.bfloat16)],
    )
    up_own = up_scatter.last()
    both_sums = scatter_last(jnp.concatenate([up_own, out_own], axis=1))
    up_sum, out_sum = both_sums[:, : up_own.shape[1]], both_sums[:, up_own.shape[1] :]
    own, other = partial_sums([plan.wait(grad_projected)], [in_low])
    plan.before = [other]
    plan.close(*plan.before, down_sum, gate_sum, layer_out)

    in_scatter.turn()
    in_scatter.send_turned()
    input_grad, sum_g_attn = row_kernel(
        functools.partial(incoming_back_kernel, mixed_order),
        [own, shift(plan.now(other), "core", 1), hidden_own, grad_residual, gain_attn],
        [(tokens, jnp.float32), (1, jnp.float32)],
    )
    sum_gains = jnp.concatenate(
        [from_gathered(sum_g_attn[0]), from_gathered(sum_g_mlp[0]), sum_g_query, sum_g_key]
    )
    gain_grad = jnp.sum(
        lax.all_to_all(
            plan.now(sum_gains).reshape(devices, -1),
            EVERY,
            split_axis=0,
            concat_axis=0,
            tiled=True,
        ),
        axis=0,
    )
    down_grad = own_rows(plan.now(down_sum), core, [down_span])
    plan.close()

    in_sum = scatter_last(after(in_scatter.last(), both_sums))
    if not mixed_order:
        layer_out, input_grad = from_gathered(layer_out), from_gathered(input_grad)

    rate = 1.0 / math.sqrt(MODEL_WIDTH)
    out_rate = 8.0 / math.sqrt(QUERY_HEADS * HEAD_SIZE)
    down_rate = 1.0 / math.sqrt(FF)
    gate_grad = own_rows(
        jnp.concatenate([gate_sum, up_sum], axis=1), core, [gate_span, up_span]
    )
    gate_new = adamw_update(gate_up, gate_grad, gate_first, gate_second, rate, weight_decay)
    down_new = adamw_update(down_proj, down_grad, down_first, down_second, down_rate, weight_decay)
    out_grad = own_rows(out_sum, core, [out_span])
    out_new = adamw_update(out_proj, out_grad, out_first, out_second, out_rate, weight_decay)
    in_grad = own_rows(in_sum, core, in_spans)
    in_new = adamw_update(
        input_projection, in_grad, input_first_moment, input_second_moment, rate, weight_decay
    )
    gain_new = adamw_update(gains, gain_grad, gain_first, gain_second, 0.5, 0.0)
    return (
        layer_out[None],
        input_grad[None],
        *in_new,
        *out_new,
        *gate_new,
        *down_new,
        *gain_new,
    )


def solution(mesh):
    dp, seq = mesh.devices.shape
    chips = Mesh(mesh.devices.reshape(dp // (COLUMNS * CORES), COLUMNS, CORES, seq), EVERY)
    tokens = P(("row", "col", "core"), "seq", None)
    places = P(("row", "col", "core"), "seq")
    weight = P(EVERY, None)
    gain = P(EVERY)
    return jax.shard_map(
        per_device,
        mesh=chips,
        in_specs=(tokens, places, tokens) + (weight,) * 4 + (gain,) + (weight,) * 8 + (gain,) * 2,
        out_specs=(tokens, tokens) + (weight,) * 12 + (gain,) * 3,
        check_vma=False,
    )
```
